32 devices in a mesh: grp: 2 (over y), wide: 8 (over z, x), narrow: 2 (over core).
Axes of the slice: x: 2, y: 2, z: 4, core: 2. Of those that a mesh axis runs over, the one named last changes fastest.
Arguments:
- frames: bfloat16 [32, 8192], P(('grp', 'wide')), parts along dimension 0, may hold values from -6 to 6
- gate_weight: bfloat16 [8192, 26624], P('narrow', 'wide'), may hold values from -0.0625 to 0.0625
- up_weight: bfloat16 [8192, 26624], P('narrow', 'wide'), may hold values from -0.0625 to 0.0625
- down_weight: bfloat16 [26624, 8192], P('wide', 'narrow'), may hold values from -0.0546875 to 0.0546875
Outputs:
- mixed: bfloat16 [32, 8192], P(('grp', 'wide'), 'narrow'), parts along dimension 0
The draws below stay inside these ranges and needn't reach their ends.
There are 2 independent parts, one for each index of `grp`. The reference program is written for one: setup_inputs(seed, part) draws one part's arguments, and reference() takes and returns one part's arrays. A program takes and returns all parts, laid end to end along the dimension named above; an argument that names none is the same for every part. Nothing has to cross between parts.
All inputs are finite; a program needn't handle non-finite values.
Results may differ from the reference program's by a relative error of at most 0.0051.
Values may be sent and summed in bfloat16 or wider, within the bound.
A program may use at most 384 MiB of HBM per device.

```python
import jax
import jax.numpy as jnp

D = 8192
FF = 26624
TOKENS = 16


def strengthened(array, own_key, source, target, shards_of, factor):
    owner, partner = [(jnp.arange(array.shape[position]) // (array.shape[position] // shards_of)).reshape([-1 if axis == position else 1 for axis in range(array.ndim)]) for position in (source, target)]
    chosen = jax.random.permutation(own_key, shards_of)[partner]
    strong = (owner == chosen) | (owner == (partner + shards_of // 2) % shards_of)
    return jnp.where(strong, factor * array, array)


def block_levels(stream_key, shape, shards, low, largest):
    factor_of, own = 1.0, jax.random.fold_in(stream_key, 6)
    for position, blocks in shards:
        heights = jnp.exp(jax.random.uniform(jax.random.fold_in(own, position), (blocks,), jnp.float32, low / len(shards), largest / len(shards)))
        factor_of = factor_of * jnp.repeat(heights, shape[position] // blocks).reshape([-1 if axis == position else 1 for axis in range(len(shape))])
    return factor_of


def noise(rng, dims, scale, reach, split=(), held_as=jnp.bfloat16):
    values = jax.random.normal(rng, dims, jnp.float32) * scale
    if len(split) > 0:
        values = block_levels(rng, dims, split, -0.22, 0.18) * values
    return jnp.clip(values, min=-reach, max=reach).astype(held_as)


def heavy_noise(key, shape, deviation, limit, cuts, heavy, dtype=jnp.bfloat16):
    entries = deviation * jax.random.normal(key, shape, jnp.float32)
    if cuts:
        entries = entries * block_levels(key, shape, cuts, -0.22, 0.18)
    return jnp.clip(strengthened(entries, jax.random.fold_in(key, 3), *heavy), -limit, limit).astype(dtype)


def setup_inputs(seed: int = 0, part: int = 0) -> dict:
    splits = jax.random.split(jax.random.key(seed), 5)
    part_splits = jax.random.split(jax.random.fold_in(splits[4], part), 5)
    frames = noise(part_splits[0], (TOKENS, D), 1.0, 6.0, ((0, 8),))
    gate_weight = noise(splits[1], (D, FF), D ** -0.5, 0.0625, ((0, 2), (1, 8)))
    up_weight = noise(splits[2], (D, FF), D ** -0.5, 0.0625, ((0, 2), (1, 8)))
    down_weight = heavy_noise(splits[3], (FF, D), FF ** -0.5, 0.0546875, ((0, 8), (1, 2)), (0, 1, 8, 2.0))
    return {"frames": frames, "gate_weight": gate_weight, "up_weight": up_weight, "down_weight": down_weight}


def reference(frames, gate_weight, up_weight, down_weight):
    gate = jnp.dot(frames, gate_weight, preferred_element_type=jnp.float32)
    up = jnp.dot(frames, up_weight, preferred_element_type=jnp.float32)
    hidden = (jax.nn.silu(gate) * up).astype(jnp.bfloat16)
    mixed = jnp.dot(hidden, down_weight, preferred_element_type=jnp.float32)
    return mixed.astype(jnp.bfloat16)
```

```python
import functools

import jax
import jax.numpy as jnp
from jax import lax
from jax.experimental import pallas as pl
from jax.experimental.pallas import tpu as pltpu
from jax.sharding import PartitionSpec as P

MESH = pl.DeviceIdType.MESH
F32 = jnp.float32
BF16 = jnp.bfloat16
LANES = 128


def kernel(
    n_grp, n_wide, inner, n_col,
    frames, gate_w, up_w, down_w, out,
    xg, xbuf, gu, dn, part, peer_part, hid, peer_hid, acc, sbuf, rbuf,
    x_local_sem, x_send_sem, fwd_send_sem, x_recv_sem, gu_sem, dn_sem,
    nar_send, nar_recv, hid_send, hid_recv, out_send, out_recv,
):
    g = lax.axis_index("grp")
    w = lax.axis_index("wide")
    n = lax.axis_index("narrow")
    half = gate_w.shape[0]
    units = gate_w.shape[1] // n_grp
    chunks = units // LANES
    cols_half = down_w.shape[1] // n_grp
    cols = cols_half // n_col
    rows = frames.shape[0]
    outer = n_wide // inner
    wo, wi = w // inner, lax.rem(w, inner)
    me = g * n_wide + w
    base = pl.multiple_of(g * units, LANES)
    other = pl.multiple_of((n_grp - 1 - g) * units, LANES)
    my_cols = pl.multiple_of(g * cols_half, LANES)

    def gu_copies(j):
        at = pl.multiple_of(base + j * LANES, LANES)
        return [
            pltpu.make_async_copy(
                m.at[:, pl.ds(at, LANES)], gu.at[j, :, pl.ds(k * LANES, LANES)], gu_sem.at[k, j]
            )
            for k, m in enumerate((gate_w, up_w))
        ]

    def dn_copies(j):
        return [
            pltpu.make_async_copy(
                down_w.at[pl.ds(pl.multiple_of(b + j * LANES, LANES), LANES), pl.ds(my_cols, cols_half)],
                dn.at[j, pl.ds(k * LANES, LANES), :],
                dn_sem.at[k, j],
            )
            for k, b in enumerate((base, other))
        ]

    @pl.loop(0, chunks)
    def _(j):
        for c in gu_copies(j):
            c.start()

    @pl.loop(0, chunks)
    def _(j):
        for c in dn_copies(j):
            c.start()

    barrier = pltpu.get_barrier_semaphore()
    peers = n_grp * n_wide

    def device(s):
        return {"grp": s // n_wide, "wide": lax.rem(s, n_wide), "narrow": n}

    @pl.loop(1, peers)
    def _(d):
        pl.semaphore_signal(barrier, inc=1, device_id=device(lax.rem(me + d, peers)), device_id_type=MESH)

    pl.semaphore_signal(barrier, inc=1, device_id={"narrow": 1 - n}, device_id_type=MESH)
    pl.semaphore_wait(barrier, peers)

    my_x = frames.at[:, pl.ds(pl.multiple_of(n * half, LANES), half)]

    def x_copy(src, s, sem, dev):
        return pltpu.make_async_remote_copy(
            src_ref=src, dst_ref=xg.at[s], send_sem=sem, recv_sem=x_recv_sem.at[s],
            device_id=dev, device_id_type=MESH,
        )

    plane = [(dg, di) for dg in range(n_grp) for di in range(inner) if dg or di]

    def plane_device(dg, di):
        return {
            "grp": lax.rem(g + dg, n_grp),
            "wide": wo * inner + lax.rem(wi + di, inner),
            "narrow": n,
        }

    def outer_slot(d):
        return g * n_wide + lax.rem(wo + d, outer) * inner + wi

    sends = []
    for d in range(1, outer):
        sends.append(x_copy(my_x, me, x_send_sem.at[d - 1], device(outer_slot(d))))
    for k, (dg, di) in enumerate(plane):
        sends.append(x_copy(my_x, me, x_send_sem.at[outer - 1 + k], plane_device(dg, di)))
    for c in sends:
        c.start()
    local = pltpu.make_async_copy(my_x, xg.at[me], x_local_sem)
    local.start()
    for d in range(1, outer):
        s = outer_slot(d)
        x_copy(my_x, s, x_send_sem.at[0], device(s)).wait_recv()
        for k, (dg, di) in enumerate(plane):
            c = x_copy(xg.at[s], s, fwd_send_sem.at[(d - 1) * len(plane) + k], plane_device(dg, di))
            c.start()
            sends.append(c)
    local.wait()
    for dg, di in plane:
        for d in range(outer):
            s = lax.rem(g + dg, n_grp) * n_wide + lax.rem(wo + d, outer) * inner + lax.rem(wi + di, inner)
            x_copy(my_x, s, x_send_sem.at[0], device(s)).wait_recv()
    for s in range(peers):
        xbuf[s * rows : (s + 1) * rows, :] = xg[s]

    def nar_copy(j):
        return pltpu.make_async_remote_copy(
            src_ref=part.at[j], dst_ref=peer_part.at[j], send_sem=nar_send.at[j], recv_sem=nar_recv.at[j],
            device_id={"narrow": 1 - n}, device_id_type=MESH,
        )

    def hid_copy(j):
        return pltpu.make_async_remote_copy(
            src_ref=hid.at[j], dst_ref=peer_hid.at[j], send_sem=hid_send.at[j], recv_sem=hid_recv.at[j],
            device_id={"grp": n_grp - 1 - g}, device_id_type=MESH,
        )

    def project(j):
        for c in gu_copies(j):
            c.wait()
        part[j] = jnp.dot(xbuf[...], gu[j], preferred_element_type=F32)
        nar_copy(j).start()

    def activate(j):
        nar_copy(j).wait_recv()
        both = part[j] + peer_part[j]
        gate, up = both[:, :LANES], both[:, LANES:]
        hid[j] = (gate / (1.0 + jnp.exp(-gate)) * up).astype(BF16)
        hid_copy(j).start()

    project(0)

    @pl.loop(1, chunks)
    def _(j):
        project(j)
        activate(j - 1)

    early = chunks - 2

    def down(c, js):
        total = None
        for j in js:
            lhs = jnp.concatenate([hid[j], peer_hid[j]], axis=1)
            term = jnp.dot(lhs, dn[j, :, c * cols : (c + 1) * cols], preferred_element_type=F32)
            total = term if total is None else total + term
        return total

    for j in range(early):
        hid_copy(j).wait_recv()
        for c in dn_copies(j):
            c.wait()
    acc[0] = down(0, range(early))
    activate(chunks - 1)
    for c in range(1, n_col):
        acc[c] = down(c, range(early))
    for j in range(early, chunks):
        hid_copy(j).wait_recv()
        for c in dn_copies(j):
            c.wait()

    def out_copy(c, d):
        s = lax.rem(me + d, peers)
        return pltpu.make_async_remote_copy(
            src_ref=sbuf.at[c, s], dst_ref=rbuf.at[c, me],
            send_sem=out_send.at[c, d], recv_sem=out_recv.at[c, me],
            device_id=device(s), device_id_type=MESH,
        )

    def out_arrival(c, d):
        s = lax.rem(me + d, peers)
        return pltpu.make_async_remote_copy(
            src_ref=sbuf.at[c, s], dst_ref=rbuf.at[c, s],
            send_sem=out_send.at[c, d], recv_sem=out_recv.at[c, s],
            device_id=device(s), device_id_type=MESH,
        )

    for c in range(n_col):
        total = acc[c] + down(c, range(early, chunks))
        for s in range(peers):
            sbuf[c, s] = total[s * rows : (s + 1) * rows, :].astype(BF16)

        @pl.loop(1, peers)
        def _(d):
            out_copy(c, d).start()

        rbuf[c, me] = sbuf[c, me]

    for c in range(n_col):
        @pl.loop(1, peers)
        def _(d):
            out_arrival(c, d).wait_recv()

        for k in range(n_grp):
            total = rbuf[c, k * n_wide].astype(F32)
            for i in range(1, n_wide):
                total = total + rbuf[c, k * n_wide + i].astype(F32)
            at = k * cols_half + c * cols
            out[:, at : at + cols] = total.astype(BF16)

    for c in sends:
        c.wait_send()

    @pl.loop(0, chunks)
    def _(j):
        nar_copy(j).wait_send()
        hid_copy(j).wait_send()

    for c in range(n_col):
        @pl.loop(1, peers)
        def _(d):
            out_copy(c, d).wait_send()


def fused(n_grp, n_wide, inner, n_col, frames, gate_w, up_w, down_w):
    half = gate_w.shape[0]
    units = gate_w.shape[1] // n_grp
    chunks = units // LANES
    width = down_w.shape[1]
    cols_half = width // n_grp
    cols = cols_half // n_col
    rows = frames.shape[0]
    peers = n_grp * n_wide
    tokens = rows * peers
    outer = n_wide // inner
    plane = n_grp * inner - 1
    dma = pltpu.SemaphoreType.DMA
    return pl.pallas_call(
        functools.partial(kernel, n_grp, n_wide, inner, n_col),
        out_shape=jax.ShapeDtypeStruct((rows, width), BF16),
        in_specs=[pl.BlockSpec(memory_space=pl.ANY)] * 4,
        out_specs=pl.BlockSpec(memory_space=pltpu.VMEM),
        scratch_shapes=[
            pltpu.VMEM((peers, rows, half), BF16),
            pltpu.VMEM((tokens, half), BF16),
            pltpu.VMEM((chunks, half, 2 * LANES), BF16),
            pltpu.VMEM((chunks, 2 * LANES, cols_half), BF16),
            pltpu.VMEM((chunks, tokens, 2 * LANES), F32),
            pltpu.VMEM((chunks, tokens, 2 * LANES), F32),
            pltpu.VMEM((chunks, tokens, LANES), BF16),
            pltpu.VMEM((chunks, tokens, LANES), BF16),
            pltpu.VMEM((n_col, tokens, cols), F32),
            pltpu.VMEM((n_col, peers, rows, cols), BF16),
            pltpu.VMEM((n_col, peers, rows, cols), BF16),
            dma,
            dma((outer - 1 + plane,)),
            dma(((outer - 1) * plane,)),
            dma((peers,)),
            dma((2, chunks)),
            dma((2, chunks)),
            dma((chunks,)),
            dma((chunks,)),
            dma((chunks,)),
            dma((chunks,)),
            dma((n_col, peers)),
            dma((n_col, peers)),
        ],
        compiler_params=pltpu.CompilerParams(
            collective_id=0, has_side_effects=True, vmem_limit_bytes=60 * 1024 * 1024
        ),
        cost_estimate=pl.CostEstimate(
            flops=2 * tokens * 3 * half * units, bytes_accessed=6 * half * units, transcendentals=tokens * units
        ),
    )(frames, gate_w, up_w, down_w)


def plain(frames, gate_weight, up_weight, down_weight):
    local_units = gate_weight.shape[1]
    half_width = gate_weight.shape[0]
    position = lax.axis_index("narrow")
    my_half = lax.dynamic_slice_in_dim(frames, position * half_width, half_width, 1)
    piece = lax.all_gather(my_half, "wide", axis=0, tiled=True)
    partial_pair = jnp.concatenate(
        [
            jnp.dot(piece, gate_weight, preferred_element_type=F32),
            jnp.dot(piece, up_weight, preferred_element_type=F32),
        ],
        axis=1,
    )
    paired = lax.psum(partial_pair, "narrow")
    gate = paired[:, :local_units]
    up_part = paired[:, local_units:]
    hidden = (jax.nn.silu(gate) * up_part).astype(BF16)
    mixed = lax.psum_scatter(
        jnp.dot(hidden, down_weight, preferred_element_type=F32),
        "wide",
        scatter_dimension=0,
        tiled=True,
    )
    return mixed.astype(BF16)


def solution(mesh):
    n_grp, n_wide, n_narrow = (mesh.shape[a] for a in ("grp", "wide", "narrow"))

    def on_device(frames, gate_weight, up_weight, down_weight):
        half, units = gate_weight.shape
        fits = (
            n_grp == 2
            and n_narrow == 2
            and n_wide % 2 == 0
            and n_wide > 2
            and units % (n_grp * LANES) == 0
            and units // (n_grp * LANES) > 2
            and 3 * half * units <= 42 * 1024 * 1024
            and n_grp * n_wide * frames.shape[0] <= 32
        )
        if fits:
            return fused(n_grp, n_wide, 2, 2, frames, gate_weight, up_weight, down_weight)
        return plain(frames, gate_weight, up_weight, down_weight)

    placed = (
        P(("grp", "wide"), None),
        P("narrow", "wide"),
        P("narrow", "wide"),
        P("wide", "narrow"),
    )
    return jax.shard_map(
        on_device,
        mesh=mesh,
        in_specs=placed,
        out_specs=P(("grp", "wide"), "narrow"),
        check_vma=False,
    )
```

```python
import functools

import jax
import jax.numpy as jnp
from jax import lax
from jax.experimental import pallas as pl
from jax.experimental.pallas import tpu as pltpu
from jax.sharding import PartitionSpec as P

MESH = pl.DeviceIdType.MESH
F32 = jnp.float32
BF16 = jnp.bfloat16
LANES = 128
LAG = 3


def kernel(
    n_grp, n_wide, inner, n_col,
    frames, gate_w, up_w, down_w, out,
    xg, xbuf, gu, dn, part, peer_part, hid, peer_hid, acc, sbuf, rbuf,
    x_local_sem, x_send_sem, fwd_send_sem, x_recv_sem, gu_sem, dn_sem,
    nar_send, nar_recv, hid_send, hid_recv, out_send, out_recv,
):
    g = lax.axis_index("grp")
    w = lax.axis_index("wide")
    n = lax.axis_index("narrow")
    half = gate_w.shape[0]
    units = gate_w.shape[1] // n_grp
    chunks = units // LANES
    cols_half = down_w.shape[1] // n_grp
    cols = cols_half // n_col
    rows = frames.shape[0]
    outer = n_wide // inner
    wo, wi = w // inner, lax.rem(w, inner)
    me = g * n_wide + w
    base = pl.multiple_of(g * units, LANES)
    other = pl.multiple_of((n_grp - 1 - g) * units, LANES)
    my_cols = pl.multiple_of(g * cols_half, LANES)

    def gu_copies(j):
        at = pl.multiple_of(base + j * LANES, LANES)
        return [
            pltpu.make_async_copy(
                m.at[:, pl.ds(at, LANES)], gu.at[j, :, pl.ds(k * LANES, LANES)], gu_sem.at[k, j]
            )
            for k, m in enumerate((gate_w, up_w))
        ]

    def dn_copies(j):
        return [
            pltpu.make_async_copy(
                down_w.at[pl.ds(pl.multiple_of(b + j * LANES, LANES), LANES), pl.ds(my_cols, cols_half)],
                dn.at[j, pl.ds(k * LANES, LANES), :],
                dn_sem.at[k, j],
            )
            for k, b in enumerate((base, other))
        ]

    barrier = pltpu.get_barrier_semaphore()
    peers = n_grp * n_wide

    def device(s):
        return {"grp": s // n_wide, "wide": lax.rem(s, n_wide), "narrow": n}

    plane = [(dg, di) for dg in range(n_grp) for di in range(inner) if dg or di]

    def plane_device(dg, di):
        return {
            "grp": lax.rem(g + dg, n_grp),
            "wide": wo * inner + lax.rem(wi + di, inner),
            "narrow": n,
        }

    def outer_slot(d):
        return g * n_wide + lax.rem(wo + d, outer) * inner + wi

    near = [device(outer_slot(d)) for d in range(1, outer)]
    near += [plane_device(dg, di) for dg, di in plane] + [{"narrow": 1 - n}]
    for dev in near:
        pl.semaphore_signal(barrier, inc=1, device_id=dev, device_id_type=MESH)

    @pl.loop(0, chunks)
    def _(j):
        for c in gu_copies(j):
            c.start()

    @pl.loop(0, chunks)
    def _(j):
        for c in dn_copies(j):
            c.start()

    pl.semaphore_wait(barrier, len(near))

    my_x = frames.at[:, pl.ds(pl.multiple_of(n * half, LANES), half)]

    def x_copy(src, s, sem, dev):
        return pltpu.make_async_remote_copy(
            src_ref=src, dst_ref=xg.at[s], send_sem=sem, recv_sem=x_recv_sem.at[s],
            device_id=dev, device_id_type=MESH,
        )

    sends = []
    for d in range(1, outer):
        sends.append(x_copy(my_x, me, x_send_sem.at[d - 1], device(outer_slot(d))))
    for k, (dg, di) in enumerate(plane):
        sends.append(x_copy(my_x, me, x_send_sem.at[outer - 1 + k], plane_device(dg, di)))
    for c in sends:
        c.start()
    local = pltpu.make_async_copy(my_x, xg.at[me], x_local_sem)
    local.start()
    for d in range(1, outer):
        s = outer_slot(d)
        x_copy(my_x, s, x_send_sem.at[0], device(s)).wait_recv()
        for k, (dg, di) in enumerate(plane):
            c = x_copy(xg.at[s], s, fwd_send_sem.at[(d - 1) * len(plane) + k], plane_device(dg, di))
            c.start()
            sends.append(c)
    local.wait()
    for dg, di in plane:
        for d in range(outer):
            s = lax.rem(g + dg, n_grp) * n_wide + lax.rem(wo + d, outer) * inner + lax.rem(wi + di, inner)
            x_copy(my_x, s, x_send_sem.at[0], device(s)).wait_recv()
    for s in range(peers):
        xbuf[s * rows : (s + 1) * rows, :] = xg[s]

    def nar_copy(j):
        return pltpu.make_async_remote_copy(
            src_ref=part.at[j], dst_ref=peer_part.at[j], send_sem=nar_send.at[j], recv_sem=nar_recv.at[j],
            device_id={"narrow": 1 - n}, device_id_type=MESH,
        )

    def hid_copy(j):
        return pltpu.make_async_remote_copy(
            src_ref=hid.at[j], dst_ref=peer_hid.at[j], send_sem=hid_send.at[j], recv_sem=hid_recv.at[j],
            device_id={"grp": n_grp - 1 - g}, device_id_type=MESH,
        )

    def project(j):
        for c in gu_copies(j):
            c.wait()
        part[j] = jnp.dot(xbuf[...], gu[j], preferred_element_type=F32)
        nar_copy(j).start()

    def activate(j):
        nar_copy(j).wait_recv()
        both = part[j] + peer_part[j]
        gate, up = both[:, :LANES], both[:, LANES:]
        hid[j] = (gate / (1.0 + jnp.exp(-gate)) * up).astype(BF16)
        hid_copy(j).start()

    for j in range(LAG):
        project(j)

    @pl.loop(LAG, chunks)
    def _(j):
        project(j)
        activate(j - LAG)

    early = chunks - LAG - 1

    def down(c, js):
        total = None
        for j in js:
            lhs = jnp.concatenate([hid[j], peer_hid[j]], axis=1)
            term = jnp.dot(lhs, dn[j, :, c * cols : (c + 1) * cols], preferred_element_type=F32)
            total = term if total is None else total + term
        return total

    for j in range(early):
        hid_copy(j).wait_recv()
        for c in dn_copies(j):
            c.wait()
    acc[0] = down(0, range(early))
    for j in range(chunks - LAG, chunks):
        activate(j)
    for c in range(1, n_col):
        acc[c] = down(c, range(early))
    for j in range(early, chunks):
        hid_copy(j).wait_recv()
        for c in dn_copies(j):
            c.wait()

    def out_copy(c, d):
        s = lax.rem(me + d, peers)
        return pltpu.make_async_remote_copy(
            src_ref=sbuf.at[c, s], dst_ref=rbuf.at[c, me],
            send_sem=out_send.at[c, d], recv_sem=out_recv.at[c, me],
            device_id=device(s), device_id_type=MESH,
        )

    def out_arrival(c, d):
        s = lax.rem(me + d, peers)
        return pltpu.make_async_remote_copy(
            src_ref=sbuf.at[c, s], dst_ref=rbuf.at[c, s],
            send_sem=out_send.at[c, d], recv_sem=out_recv.at[c, s],
            device_id=device(s), device_id_type=MESH,
        )

    for c in range(n_col):
        total = acc[c] + down(c, range(early, chunks))
        for s in range(peers):
            sbuf[c, s] = total[s * rows : (s + 1) * rows, :].astype(BF16)

        @pl.loop(1, peers)
        def _(d):
            out_copy(c, d).start()

        rbuf[c, me] = sbuf[c, me]

    for c in range(n_col):
        @pl.loop(1, peers)
        def _(d):
            out_arrival(c, d).wait_recv()

        for k in range(n_grp):
            total = rbuf[c, k * n_wide].astype(F32)
            for i in range(1, n_wide):
                total = total + rbuf[c, k * n_wide + i].astype(F32)
            at = k * cols_half + c * cols
            out[:, at : at + cols] = total.astype(BF16)

    for c in sends:
        c.wait_send()

    @pl.loop(0, chunks)
    def _(j):
        nar_copy(j).wait_send()
        hid_copy(j).wait_send()

    for c in range(n_col):
        @pl.loop(1, peers)
        def _(d):
            out_copy(c, d).wait_send()


def fused(n_grp, n_wide, inner, n_col, frames, gate_w, up_w, down_w):
    half = gate_w.shape[0]
    units = gate_w.shape[1] // n_grp
    chunks = units // LANES
    width = down_w.shape[1]
    cols_half = width // n_grp
    cols = cols_half // n_col
    rows = frames.shape[0]
    peers = n_grp * n_wide
    tokens = rows * peers
    outer = n_wide // inner
    plane = n_grp * inner - 1
    dma = pltpu.SemaphoreType.DMA
    return pl.pallas_call(
        functools.partial(kernel, n_grp, n_wide, inner, n_col),
        out_shape=jax.ShapeDtypeStruct((rows, width), BF16),
        in_specs=[pl.BlockSpec(memory_space=pl.ANY)] * 4,
        out_specs=pl.BlockSpec(memory_space=pltpu.VMEM),
        scratch_shapes=[
            pltpu.VMEM((peers, rows, half), BF16),
            pltpu.VMEM((tokens, half), BF16),
            pltpu.VMEM((chunks, half, 2 * LANES), BF16),
            pltpu.VMEM((chunks, 2 * LANES, cols_half), BF16),
            pltpu.VMEM((chunks, tokens, 2 * LANES), F32),
            pltpu.VMEM((chunks, tokens, 2 * LANES), F32),
            pltpu.VMEM((chunks, tokens, LANES), BF16),
            pltpu.VMEM((chunks, tokens, LANES), BF16),
            pltpu.VMEM((n_col, tokens, cols), F32),
            pltpu.VMEM((n_col, peers, rows, cols), BF16),
            pltpu.VMEM((n_col, peers, rows, cols), BF16),
            dma,
            dma((outer - 1 + plane,)),
            dma(((outer - 1) * plane,)),
            dma((peers,)),
            dma((2, chunks)),
            dma((2, chunks)),
            dma((chunks,)),
            dma((chunks,)),
            dma((chunks,)),
            dma((chunks,)),
            dma((n_col, peers)),
            dma((n_col, peers)),
        ],
        compiler_params=pltpu.CompilerParams(
            collective_id=0, has_side_effects=True, vmem_limit_bytes=60 * 1024 * 1024
        ),
        cost_estimate=pl.CostEstimate(
            flops=2 * tokens * 3 * half * units, bytes_accessed=6 * half * units, transcendentals=tokens * units
        ),
    )(frames, gate_w, up_w, down_w)


def plain(frames, gate_weight, up_weight, down_weight):
    local_units = gate_weight.shape[1]
    half_width = gate_weight.shape[0]
    position = lax.axis_index("narrow")
    my_half = lax.dynamic_slice_in_dim(frames, position * half_width, half_width, 1)
    piece = lax.all_gather(my_half, "wide", axis=0, tiled=True)
    partial_pair = jnp.concatenate(
        [
            jnp.dot(piece, gate_weight, preferred_element_type=F32),
            jnp.dot(piece, up_weight, preferred_element_type=F32),
        ],
        axis=1,
    )
    paired = lax.psum(partial_pair, "narrow")
    gate = paired[:, :local_units]
    up_part = paired[:, local_units:]
    hidden = (jax.nn.silu(gate) * up_part).astype(BF16)
    mixed = lax.psum_scatter(
        jnp.dot(hidden, down_weight, preferred_element_type=F32),
        "wide",
        scatter_dimension=0,
        tiled=True,
    )
    return mixed.astype(BF16)


def solution(mesh):
    n_grp, n_wide, n_narrow = (mesh.shape[a] for a in ("grp", "wide", "narrow"))

    def on_device(frames, gate_weight, up_weight, down_weight):
        half, units = gate_weight.shape
        fits = (
            n_grp == 2
            and n_narrow == 2
            and n_wide % 2 == 0
            and n_wide > 2
            and units % (n_grp * LANES) == 0
            and units // (n_grp * LANES) > LAG + 1
            and 3 * half * units <= 42 * 1024 * 1024
            and n_grp * n_wide * frames.shape[0] <= 32
        )
        if fits:
            return fused(n_grp, n_wide, 2, 2, frames, gate_weight, up_weight, down_weight)
        return plain(frames, gate_weight, up_weight, down_weight)

    placed = (
        P(("grp", "wide"), None),
        P("narrow", "wide"),
        P("narrow", "wide"),
        P("wide", "narrow"),
    )
    return jax.shard_map(
        on_device,
        mesh=mesh,
        in_specs=placed,
        out_specs=P(("grp", "wide"), "narrow"),
        check_vma=False,
    )
```

```python
import functools

import jax
import jax.numpy as jnp
from jax import lax
from jax.experimental import pallas as pl
from jax.experimental.pallas import tpu as pltpu
from jax.sharding import PartitionSpec as P

MESH = pl.DeviceIdType.MESH
F32 = jnp.float32
BF16 = jnp.bfloat16
LANES = 128
LAG = 3


def kernel(
    n_grp, n_wide, inner, n_col,
    frames, gate_w, up_w, down_w, out,
    xg, xbuf, gu, dn, part, peer_part, hid, peer_hid, acc, sbuf, rbuf,
    x_local_sem, x_send_sem, fwd_send_sem, x_recv_sem, gu_sem, dn_sem,
    nar_send, nar_recv, hid_send, hid_recv, out_send, out_recv,
):
    g = lax.axis_index("grp")
    w = lax.axis_index("wide")
    n = lax.axis_index("narrow")
    half = gate_w.shape[0]
    units = gate_w.shape[1] // n_grp
    chunks = units // LANES
    cols_half = down_w.shape[1] // n_grp
    cols = cols_half // n_col
    rows = frames.shape[0]
    outer = n_wide // inner
    wo, wi = w // inner, lax.rem(w, inner)
    me = g * n_wide + w
    base = pl.multiple_of(g * units, LANES)
    other = pl.multiple_of((n_grp - 1 - g) * units, LANES)
    my_cols = pl.multiple_of(g * cols_half, LANES)

    def gu_copies(j):
        at = pl.multiple_of(base + j * LANES, LANES)
        return [
            pltpu.make_async_copy(
                m.at[:, pl.ds(at, LANES)], gu.at[j, :, pl.ds(k * LANES, LANES)], gu_sem.at[k, j]
            )
            for k, m in enumerate((gate_w, up_w))
        ]

    def dn_copies(j):
        return [
            pltpu.make_async_copy(
                down_w.at[pl.ds(pl.multiple_of(b + j * LANES, LANES), LANES), pl.ds(my_cols, cols_half)],
                dn.at[j, pl.ds(k * LANES, LANES), :],
                dn_sem.at[k, j],
            )
            for k, b in enumerate((base, other))
        ]

    barrier = pltpu.get_barrier_semaphore()
    peers = n_grp * n_wide

    def device(s):
        return {"grp": s // n_wide, "wide": lax.rem(s, n_wide), "narrow": n}

    plane = [(dg, di) for dg in range(n_grp) for di in range(inner) if dg or di]

    def plane_device(dg, di):
        return {
            "grp": lax.rem(g + dg, n_grp),
            "wide": wo * inner + lax.rem(wi + di, inner),
            "narrow": n,
        }

    def outer_slot(d):
        return g * n_wide + lax.rem(wo + d, outer) * inner + wi

    near = [device(outer_slot(d)) for d in range(1, outer)]
    near += [plane_device(dg, di) for dg, di in plane] + [{"narrow": 1 - n}]
    for dev in near:
        pl.semaphore_signal(barrier, inc=1, device_id=dev, device_id_type=MESH)

    @pl.loop(0, chunks)
    def _(j):
        for c in gu_copies(j):
            c.start()

    @pl.loop(0, chunks)
    def _(j):
        for c in dn_copies(j):
            c.start()

    pl.semaphore_wait(barrier, len(near))

    my_x = frames.at[:, pl.ds(pl.multiple_of(n * half, LANES), half)]

    def x_copy(src, s, sem, dev):
        return pltpu.make_async_remote_copy(
            src_ref=src, dst_ref=xg.at[s], send_sem=sem, recv_sem=x_recv_sem.at[s],
            device_id=dev, device_id_type=MESH,
        )

    sends = []
    for d in range(1, outer):
        sends.append(x_copy(my_x, me, x_send_sem.at[d - 1], device(outer_slot(d))))
    for k, (dg, di) in enumerate(plane):
        sends.append(x_copy(my_x, me, x_send_sem.at[outer - 1 + k], plane_device(dg, di)))
    for c in sends:
        c.start()
    local = pltpu.make_async_copy(my_x, xg.at[me], x_local_sem)
    local.start()
    for d in range(1, outer):
        s = outer_slot(d)
        x_copy(my_x, s, x_send_sem.at[0], device(s)).wait_recv()
        for k, (dg, di) in enumerate(plane):
            c = x_copy(xg.at[s], s, fwd_send_sem.at[(d - 1) * len(plane) + k], plane_device(dg, di))
            c.start()
            sends.append(c)
    local.wait()
    for dg, di in plane:
        for d in range(outer):
            s = lax.rem(g + dg, n_grp) * n_wide + lax.rem(wo + d, outer) * inner + lax.rem(wi + di, inner)
            x_copy(my_x, s, x_send_sem.at[0], device(s)).wait_recv()
    for s in range(peers):
        xbuf[s * rows : (s + 1) * rows, :] = xg[s]

    def nar_copy(j):
        return pltpu.make_async_remote_copy(
            src_ref=part.at[j], dst_ref=peer_part.at[j], send_sem=nar_send.at[j], recv_sem=nar_recv.at[j],
            device_id={"narrow": 1 - n}, device_id_type=MESH,
        )

    def hid_copy(j):
        return pltpu.make_async_remote_copy(
            src_ref=hid.at[j], dst_ref=peer_hid.at[j], send_sem=hid_send.at[j], recv_sem=hid_recv.at[j],
            device_id={"grp": n_grp - 1 - g}, device_id_type=MESH,
        )

    def project(j):
        for c in gu_copies(j):
            c.wait()
        part[j] = jnp.dot(xbuf[...], gu[j], preferred_element_type=F32)
        nar_copy(j).start()

    def activate(j):
        nar_copy(j).wait_recv()
        both = part[j] + peer_part[j]
        gate, up = both[:, :LANES], both[:, LANES:]
        hid[j] = (gate / (1.0 + jnp.exp(-gate)) * up).astype(BF16)
        hid_copy(j).start()

    for j in range(LAG):
        project(j)

    @pl.loop(LAG, chunks)
    def _(j):
        project(j)
        activate(j - LAG)

    early = chunks - LAG - 1

    def down(c, js):
        total = None
        for j in js:
            lhs = jnp.concatenate([hid[j], peer_hid[j]], axis=1)
            term = jnp.dot(lhs, dn[j, :, c * cols : (c + 1) * cols], preferred_element_type=F32)
            total = term if total is None else total + term
        return total

    for j in range(chunks - LAG, chunks):
        activate(j)

    for j in range(early):
        hid_copy(j).wait_recv()
        for c in dn_copies(j):
            c.wait()
    acc[0] = down(0, range(early))
    for c in range(1, n_col):
        acc[c] = down(c, range(early))
    for j in range(early, chunks):
        hid_copy(j).wait_recv()
        for c in dn_copies(j):
            c.wait()

    def out_copy(c, d):
        s = lax.rem(me + d, peers)
        return pltpu.make_async_remote_copy(
            src_ref=sbuf.at[c, s], dst_ref=rbuf.at[c, me],
            send_sem=out_send.at[c, d], recv_sem=out_recv.at[c, me],
            device_id=device(s), device_id_type=MESH,
        )

    def out_arrival(c, d):
        s = lax.rem(me + d, peers)
        return pltpu.make_async_remote_copy(
            src_ref=sbuf.at[c, s], dst_ref=rbuf.at[c, s],
            send_sem=out_send.at[c, d], recv_sem=out_recv.at[c, s],
            device_id=device(s), device_id_type=MESH,
        )

    for c in range(n_col):
        total = acc[c] + down(c, range(early, chunks))
        for s in range(peers):
            sbuf[c, s] = total[s * rows : (s + 1) * rows, :].astype(BF16)

        @pl.loop(1, peers)
        def _(d):
            out_copy(c, d).start()

        rbuf[c, me] = sbuf[c, me]

    for c in range(n_col):
        @pl.loop(1, peers)
        def _(d):
            out_arrival(c, d).wait_recv()

        for k in range(n_grp):
            total = rbuf[c, k * n_wide].astype(F32)
            for i in range(1, n_wide):
                total = total + rbuf[c, k * n_wide + i].astype(F32)
            at = k * cols_half + c * cols
            out[:, at : at + cols] = total.astype(BF16)

    for c in sends:
        c.wait_send()

    @pl.loop(0, chunks)
    def _(j):
        nar_copy(j).wait_send()
        hid_copy(j).wait_send()

    for c in range(n_col):
        @pl.loop(1, peers)
        def _(d):
            out_copy(c, d).wait_send()


def fused(n_grp, n_wide, inner, n_col, frames, gate_w, up_w, down_w):
    half = gate_w.shape[0]
    units = gate_w.shape[1] // n_grp
    chunks = units // LANES
    width = down_w.shape[1]
    cols_half = width // n_grp
    cols = cols_half // n_col
    rows = frames.shape[0]
    peers = n_grp * n_wide
    tokens = rows * peers
    outer = n_wide // inner
    plane = n_grp * inner - 1
    dma = pltpu.SemaphoreType.DMA
    return pl.pallas_call(
        functools.partial(kernel, n_grp, n_wide, inner, n_col),
        out_shape=jax.ShapeDtypeStruct((rows, width), BF16),
        in_specs=[pl.BlockSpec(memory_space=pl.ANY)] * 4,
        out_specs=pl.BlockSpec(memory_space=pltpu.VMEM),
        scratch_shapes=[
            pltpu.VMEM((peers, rows, half), BF16),
            pltpu.VMEM((tokens, half), BF16),
            pltpu.VMEM((chunks, half, 2 * LANES), BF16),
            pltpu.VMEM((chunks, 2 * LANES, cols_half), BF16),
            pltpu.VMEM((chunks, tokens, 2 * LANES), F32),
            pltpu.VMEM((chunks, tokens, 2 * LANES), F32),
            pltpu.VMEM((chunks, tokens, LANES), BF16),
            pltpu.VMEM((chunks, tokens, LANES), BF16),
            pltpu.VMEM((n_col, tokens, cols), F32),
            pltpu.VMEM((n_col, peers, rows, cols), BF16),
            pltpu.VMEM((n_col, peers, rows, cols), BF16),
            dma,
            dma((outer - 1 + plane,)),
            dma(((outer - 1) * plane,)),
            dma((peers,)),
            dma((2, chunks)),
            dma((2, chunks)),
            dma((chunks,)),
            dma((chunks,)),
            dma((chunks,)),
            dma((chunks,)),
            dma((n_col, peers)),
            dma((n_col, peers)),
        ],
        compiler_params=pltpu.CompilerParams(
            collective_id=0, has_side_effects=True, vmem_limit_bytes=60 * 1024 * 1024
        ),
        cost_estimate=pl.CostEstimate(
            flops=2 * tokens * 3 * half * units, bytes_accessed=6 * half * units, transcendentals=tokens * units
        ),
    )(frames, gate_w, up_w, down_w)


def plain(frames, gate_weight, up_weight, down_weight):
    local_units = gate_weight.shape[1]
    half_width = gate_weight.shape[0]
    position = lax.axis_index("narrow")
    my_half = lax.dynamic_slice_in_dim(frames, position * half_width, half_width, 1)
    piece = lax.all_gather(my_half, "wide", axis=0, tiled=True)
    partial_pair = jnp.concatenate(
        [
            jnp.dot(piece, gate_weight, preferred_element_type=F32),
            jnp.dot(piece, up_weight, preferred_element_type=F32),
        ],
        axis=1,
    )
    paired = lax.psum(partial_pair, "narrow")
    gate = paired[:, :local_units]
    up_part = paired[:, local_units:]
    hidden = (jax.nn.silu(gate) * up_part).astype(BF16)
    mixed = lax.psum_scatter(
        jnp.dot(hidden, down_weight, preferred_element_type=F32),
        "wide",
        scatter_dimension=0,
        tiled=True,
    )
    return mixed.astype(BF16)


def solution(mesh):
    n_grp, n_wide, n_narrow = (mesh.shape[a] for a in ("grp", "wide", "narrow"))

    def on_device(frames, gate_weight, up_weight, down_weight):
        half, units = gate_weight.shape
        fits = (
            n_grp == 2
            and n_narrow == 2
            and n_wide % 2 == 0
            and n_wide > 2
            and units % (n_grp * LANES) == 0
            and units // (n_grp * LANES) > LAG + 1
            and 3 * half * units <= 42 * 1024 * 1024
            and n_grp * n_wide * frames.shape[0] <= 32
        )
        if fits:
            return fused(n_grp, n_wide, 2, 1, frames, gate_weight, up_weight, down_weight)
        return plain(frames, gate_weight, up_weight, down_weight)

    placed = (
        P(("grp", "wide"), None),
        P("narrow", "wide"),
        P("narrow", "wide"),
        P("wide", "narrow"),
    )
    return jax.shard_map(
        on_device,
        mesh=mesh,
        in_specs=placed,
        out_specs=P(("grp", "wide"), "narrow"),
        check_vma=False,
    )
```
